256 devices in a mesh: orb: 8 (over z_lo, y), fft: 32 (over x, z_hi, core).
Axes of the slice: x: 4, y: 4, z: 8 (z_hi: 4, z_lo: 2; z = z_hi * 2 + z_lo), core: 2. Of those that a mesh axis runs over, the one named last changes fastest.
Arguments:
- targets: float32 [8, 128, 128, 128], P('orb', 'fft'), may hold values from -6 to 6
- occupied: float32 [8, 128, 128, 128], P('orb', 'fft'), may hold values from -6 to 6
- sphere_map: int32 [131072], P('fft'), may hold values from 0 to 65535, as said below
Outputs:
- exchange_sphere: float32 [8, 2, 131072], P('orb', None, 'fft')
The draws below stay inside these ranges and needn't reach their ends.
Inputs may be any that keep to these rules, and one draw needn't show every extreme that they name: `sphere_map`: within each aligned block of 4096 entries the entries are distinct cells of that block's spectral slab, numbered over 128 x 4 x 128 cells in that order; the block holds exactly one cell of every aligned run of 16 cells.
All inputs are finite; a program needn't handle non-finite values.
Results may differ from the reference program's by a relative error of at most 0.0001.
Values sent between devices are 32-bit elements; how exact they have to be, the bound alone decides.
No kernel may reach another device: no remote copies, remote signals or barrier semaphores. Data moves between devices by JAX's collectives and lax.ppermute only.
A program may use at most 128 MiB of HBM per device.

```python
import jax
import jax.numpy as jnp
from jax import lax

GRID = 128
SLAB = 4
TGT = 8
OCC = 8
NSPH_DEV = 4096
NSPH = 131072
N_FFT = 32


def draw_sphere_map(key, part):
    key = jax.random.fold_in(key, 7)
    slab_cells = GRID * GRID * (GRID // N_FFT)
    stride = slab_cells // NSPH_DEV
    offsets = jax.random.randint(key, (N_FFT, NSPH_DEV), 0, stride)
    offsets = offsets.at[:, 0].set(0).at[:, NSPH_DEV - 1].set(stride - 1)
    cell_ids = jnp.arange(NSPH_DEV, dtype=jnp.int32)[None, :] * stride + offsets
    order_keys = jax.random.split(jax.random.fold_in(key, 1), N_FFT)
    orders = jax.vmap(lambda subkey: jax.random.permutation(subkey, NSPH_DEV))(order_keys)
    return jnp.take_along_axis(cell_ids, orders, axis=1).reshape(-1).astype(jnp.int32)


def steps_of(rng, extent, shards, smallest, top_value):
    def one(axis_at, parts):
        steps = jax.random.uniform(jax.random.fold_in(jax.random.fold_in(rng, 6), axis_at), (parts,), jnp.float32, smallest / len(shards), top_value / len(shards))
        return jnp.repeat(jnp.exp(steps), extent[axis_at] // parts).reshape((-1,) + (1,) * (len(extent) - axis_at - 1))

    factor_of = one(*shards[0])
    for cut in shards[1:]:
        factor_of = factor_of * one(*cut)
    return factor_of


def normal_values(own_key, shape, scale, bound, shards=(), kind=jnp.bfloat16):
    drawn = jax.random.normal(own_key, shape, jnp.float32) * scale
    if len(shards) > 0:
        drawn = steps_of(own_key, shape, shards, -0.22, 0.18) * drawn
    return jnp.clip(drawn, min=-bound, max=bound).astype(kind)


def setup_inputs(seed: int = 0) -> dict:
    key_of = jax.random.split(jax.random.key(seed), 4)
    return {
        "targets": normal_values(key_of[0], (TGT, GRID, GRID, GRID), 1.0, 6.0, ((0, 8), (1, 32)), jnp.float32),
        "occupied": normal_values(key_of[1], (OCC, GRID, GRID, GRID), 1.0, 6.0, ((0, 8), (1, 32)), jnp.float32),
        "sphere_map": draw_sphere_map(jax.random.fold_in(key_of[3], 71), 0),
    }


box_length = 82.0
screening = 0.106

def screened_kernel(grid_size, count, offset):
    counter = jnp.arange(grid_size, dtype=jnp.int32)
    folded = jnp.where(counter < grid_size // 2, counter, counter - grid_size).astype(jnp.float32)
    rows = offset + jnp.arange(count, dtype=jnp.int32)
    folded_rows = jnp.where(rows < grid_size // 2, rows, rows - grid_size).astype(jnp.float32)
    factor = (2.0 * jnp.pi / box_length) ** 2
    square_norm = factor * (folded[:, None, None] ** 2 + folded_rows[None, :, None] ** 2 + folded[None, None, :] ** 2)
    safe_square = jnp.where(square_norm > 0, square_norm, 1.0)
    screened = 4.0 * jnp.pi / safe_square * (1.0 - jnp.exp(-safe_square / (4.0 * screening * screening)))
    return jnp.where(square_norm > 0, screened, jnp.pi / (screening * screening)).astype(jnp.float32)

def reference(targets, occupied, sphere_map):
    kernel = screened_kernel(GRID, GRID, 0)

    def one_band(target_band):

        def add_term(running, occ_band):
            spectrum = jnp.fft.fftn(occ_band * target_band) * kernel
            potential = jnp.real(jnp.fft.ifftn(spectrum))
            return (running - occ_band * potential, None)
        running, _ = lax.scan(add_term, jnp.zeros((GRID, GRID, GRID), jnp.float32), occupied)
        return running
    applied = lax.map(one_band, targets)
    positions = jnp.arange(NSPH, dtype=jnp.int32)
    owner_index = positions // NSPH_DEV
    plane_index = sphere_map // (SLAB * GRID)
    row_index = sphere_map // GRID % SLAB
    depth_index = sphere_map % GRID
    cells = (plane_index * GRID * GRID + (owner_index * SLAB + row_index) * GRID + depth_index).astype(jnp.int32)
    norm_factor = 1.0 / jnp.sqrt(jnp.float32(GRID) ** 3)

    def one_spectrum(signal):
        flattened = jnp.fft.fftn(signal).reshape(-1)[cells]
        return jnp.stack([jnp.real(flattened), jnp.imag(flattened)], axis=0) * norm_factor
    return lax.map(one_spectrum, applied)
```

```python
import jax
import jax.numpy as jnp
import ml_dtypes
import numpy as np
from jax import lax
from jax.experimental import pallas as pl
from jax.experimental.pallas import tpu as pltpu
from jax.sharding import Mesh
from jax.sharding import PartitionSpec as P

box_length = 82.0
screening = 0.106
grid = 128
axes = ("zlo", "y", "x", "zhi", "core")
extent = {"zlo": 2, "y": 4, "x": 4, "zhi": 4, "core": 2}
vmem = pl.BlockSpec(memory_space=pltpu.VMEM)
smem = pl.BlockSpec(memory_space=pltpu.SMEM)
params = pltpu.CompilerParams(vmem_limit_bytes=48 * 1024 * 1024)


def split_table(table):
    high = table.astype(ml_dtypes.bfloat16)
    low = (table - high.astype(np.float64)).astype(ml_dtypes.bfloat16)
    return high, low


def waves(rows, cols):
    angles = (np.outer(rows, cols) % grid) * (2.0 * np.pi / grid)
    return np.cos(angles), np.sin(angles)


def forward_left(out_index, in_index):
    cosine, sine = waves(out_index, in_index)
    return np.block([[cosine, sine], [-sine, cosine]])


def inverse_left(out_index, in_index):
    cosine, sine = waves(out_index, in_index)
    return np.block([[cosine, -sine], [sine, cosine]])


natural = np.arange(grid)


def order_rows(block, blocks):
    index = np.arange(2 * grid).reshape(2, blocks, block)
    return index.transpose(1, 0, 2).reshape(-1)


def plane_order(turn):
    cx, core, m, p = np.meshgrid(np.arange(4), np.arange(2), np.arange(4), np.arange(4), indexing="ij")
    return (32 * cx + 8 * ((m + turn) % 4) + 4 * core + p).reshape(-1)


def interleave(count):
    return np.arange(2 * count).reshape(2, count).T.reshape(-1)


def make_tables():
    tables = {}
    tables["z"] = split_table(forward_left(natural, natural).T)
    tables["zi"] = split_table(inverse_left(natural, natural).T)
    rows = order_rows(16, 8)
    tables["y"] = split_table(forward_left(natural, natural)[rows])
    tables["yi"] = split_table(inverse_left(natural, natural)[:, rows])
    tables["y_end"] = split_table(forward_left(natural, natural)[order_rows(4, 32)])
    pairs = interleave(grid)
    forward, inverse = [], []
    for turn in range(4):
        order = plane_order(turn)
        forward.append(forward_left(natural, order)[:, pairs])
        inverse.append(inverse_left(order, natural)[pairs])
    tables["x"] = split_table(np.stack(forward))
    tables["xi"] = split_table(np.stack(inverse))
    tables["x_end"] = split_table(forward_left(natural, natural)[:, pairs])
    return tables


def halves(value):
    high = value.astype(jnp.bfloat16)
    low = (value - high.astype(jnp.float32)).astype(jnp.bfloat16)
    return high, low


def product(left, right):
    def one(a, b):
        return lax.dot_general(a, b, (((1,), (0,)), ((), ())), preferred_element_type=jnp.float32)

    return one(left[0], right[0]) + (one(left[0], right[1]) + one(left[1], right[0]))


def read(pair):
    return pair[0][...], pair[1][...]


def planes_to_columns(value):
    top = [value[p * grid : (p + 1) * grid, :grid] for p in range(4)]
    low = [value[p * grid : (p + 1) * grid, grid:] for p in range(4)]
    return jnp.concatenate([jnp.concatenate(top, axis=1), jnp.concatenate(low, axis=1)], axis=0)


def columns_to_planes(value):
    parts = []
    for p in range(4):
        block = value[:, p * grid : (p + 1) * grid]
        parts.append(jnp.concatenate([block[:grid], block[grid:]], axis=1))
    return jnp.concatenate(parts, axis=0)


def choose(index, refs):
    value = refs[0][...]
    for at in range(1, len(refs)):
        value = jnp.where(index == at, refs[at][...], value)
    return value


def occupied_of(m, parity, blocks):
    own = choose(m, [blocks[0], blocks[2], blocks[4], blocks[6]])
    after = choose(m, [blocks[1], blocks[3], blocks[5], blocks[7]])
    before = choose(m, [blocks[7], blocks[1], blocks[3], blocks[5]])
    return own, jnp.where(parity == 0, after, before)


def density_kernel(place, *refs):
    targets, blocks = refs[:4], refs[4:12]
    z_pair, y_pair, out = refs[12:14], refs[14:16], refs[16]
    z_table, y_table = read(z_pair), read(y_pair)

    def step(m, carry):
        band = choose(lax.rem(place[0] + 4 - m, 4), targets)
        own, other = occupied_of(m, place[1], blocks)
        packed = jnp.concatenate([band * own, band * other], axis=1)
        lines = product(halves(packed), z_table)
        spread = product(y_table, halves(planes_to_columns(lines)))
        for p in range(4):
            part = spread[:, p * grid : (p + 1) * grid]
            out[:, pl.ds(m, 1), pl.ds(p, 1)] = part.reshape(8, 1, 1, 32, grid)
        return carry

    lax.fori_loop(0, 4, step, 0)


def convolve_kernel(arrived, weights, x_high, x_low, xi_high, xi_low, out):
    x_table = (x_high[...], x_low[...])
    xi_table = (xi_high[...], xi_low[...])
    for pair in range(8):
        columns = [arrived[pl.ds(2 * pair + k, 2 * grid, 16), :] for k in range(2)]
        spectrum = product(x_table, halves(jnp.concatenate(columns, axis=1)))
        weight = weights[:, pl.ds(pair * 2 * grid, 2 * grid)]
        scaled = jnp.concatenate([spectrum[:grid] * weight, spectrum[grid:] * weight], axis=0)
        back = product(xi_table, halves(scaled))
        for k in range(2):
            out[pl.ds(2 * pair + k, 2 * grid, 16), :] = back[:, k * grid : (k + 1) * grid]


def field_kernel(place, arrived, *refs):
    blocks = refs[:8]
    yi_table, zi_table = read(refs[8:10]), read(refs[10:12])
    outs = refs[12:16]
    for k in range(4):
        m = lax.rem(place[2] + k, 4)
        rows = jnp.concatenate(
            [arrived[:, pl.ds(m, 1), pl.ds(p, 1)].reshape(2 * grid, grid) for p in range(4)], axis=1
        )
        lines = product(yi_table, halves(rows))
        values = product(halves(columns_to_planes(lines)), zi_table)
        own, other = occupied_of(m, place[1], blocks)
        outs[k][...] = -(own * values[:, :grid] + other * values[:, grid:])


def applied_kernel(own, one, two, three, z_high, z_low, y_high, y_low, out):
    applied = (own[...] + one[...]) + (two[...] + three[...])
    lines = product(halves(applied), (z_high[:grid], z_low[:grid]))
    spread = product((y_high[...], y_low[...]), halves(planes_to_columns(lines)))
    for p in range(4):
        out[:, pl.ds(p, 1)] = spread[:, p * grid : (p + 1) * grid].reshape(32, 1, 8, grid)


def mask_kernel(cells, out):
    cell = cells[...]
    rows = cell // grid
    row_hot = (lax.broadcasted_iota(jnp.int32, (512, 4096), 0) == rows).astype(jnp.bfloat16)
    lane_hot = (lax.broadcasted_iota(jnp.int32, (grid, 4096), 0) == cell % grid).astype(jnp.bfloat16)
    out[...] = lax.dot_general(
        row_hot, lane_hot, (((1,), (1,)), ((), ())), preferred_element_type=jnp.float32
    )


def pick_kernel(arrived, cells, mask, x_high, x_low, out):
    x_table = (x_high[...], x_low[...])
    lane = lax.broadcasted_iota(jnp.int32, (grid, grid), 0)
    group = lax.broadcasted_iota(jnp.int32, (grid, grid), 1)
    total = jnp.zeros((2 * grid, grid), jnp.float32)
    for pair in range(2):
        columns = [arrived[pl.ds(2 * pair + k, 2 * grid, 4), :] for k in range(2)]
        spectrum = product(x_table, halves(jnp.concatenate(columns, axis=1)))
        for k in range(2):
            row = 2 * pair + k
            kept = mask[pl.ds(row, grid, 4), :]
            part = spectrum[:, k * grid : (k + 1) * grid]
            part = jnp.concatenate([part[:grid] * kept, part[grid:] * kept], axis=0)
            ones = (group == row * 8 + lane // 16).astype(jnp.bfloat16)
            for piece in halves(part):
                total = total + lax.dot_general(
                    piece, ones, (((1,), (0,)), ((), ())), preferred_element_type=jnp.float32
                )
    cell = cells[...]
    plane_hot = (lax.broadcasted_iota(jnp.int32, (grid, 4096), 0) == cell // 512).astype(jnp.bfloat16)
    run_hot = lax.broadcasted_iota(jnp.int32, (32, 4096), 0) == (cell // 16) % 32
    norm = 1.0 / float(np.sqrt(float(grid) ** 3))
    for c in range(2):
        runs = total[c * grid : (c + 1) * grid].T[:32]
        spread = jnp.zeros((32, 4096), jnp.float32)
        for piece in halves(runs):
            spread = spread + lax.dot_general(
                piece, plane_hot, (((1,), (0,)), ((), ())), preferred_element_type=jnp.float32
            )
        out[pl.ds(c, 1), :] = (
            jnp.sum(jnp.where(run_hot, spread, 0.0), axis=0, keepdims=True) * norm
        )


def call(kernel, shapes, specs, *args):
    return pl.pallas_call(
        kernel, out_shape=shapes, in_specs=specs, out_specs=jax.tree.map(lambda _: vmem, shapes),
        compiler_params=params,
    )(*args)


def floats(*shape):
    return jax.ShapeDtypeStruct(shape, jnp.float32)


def moved(change):
    pairs = []
    sizes = tuple(extent[a] for a in axes)
    for at in np.ndindex(sizes):
        spot = dict(zip(axes, at))
        goal = change(dict(spot))
        pairs.append((int(np.ravel_multi_index(at, sizes)),
                      int(np.ravel_multi_index(tuple(goal[a] for a in axes), sizes))))
    return pairs


def swapped(spot):
    spot["y"], spot["zhi"] = spot["zhi"], spot["y"]
    return spot


def along_z(step):
    def change(spot):
        z = (spot["zhi"] * 2 + spot["zlo"] + step) % 8
        spot["zhi"], spot["zlo"] = z // 2, z % 2
        return spot

    return moved(change)


def along_y(step):
    def change(spot):
        spot["y"] = (spot["y"] + step) % 4
        return spot

    return moved(change)


def send(value, pairs):
    return lax.ppermute(value, axes, pairs)


def ring(block):
    blocks = {0: block}
    up = down = block
    for step in range(1, 4):
        up = send(up, along_z(1))
        down = send(down, along_z(-1))
        blocks[8 - step] = up
        blocks[step] = down
    half = block.shape[0] // 2
    blocks[4] = jnp.concatenate([send(up[:half], along_z(1)), send(down[half:], along_z(-1))])
    return [blocks[at] for at in range(8)]


def screened_weights(first_row):
    counter = jnp.arange(grid, dtype=jnp.int32)
    folded = jnp.where(counter < grid // 2, counter, counter - grid).astype(jnp.float32)
    rows = first_row + jnp.arange(16, dtype=jnp.int32)
    folded_rows = jnp.where(rows < grid // 2, rows, rows - grid).astype(jnp.float32)
    factor = (2.0 * jnp.pi / box_length) ** 2
    square_norm = factor * (
        folded[:, None, None] ** 2 + folded_rows[None, :, None] ** 2 + folded[None, None, :] ** 2
    )
    safe_square = jnp.where(square_norm > 0, square_norm, 1.0)
    screened = 4.0 * jnp.pi / safe_square * (1.0 - jnp.exp(-safe_square / (4.0 * screening * screening)))
    kernel = jnp.where(square_norm > 0, screened, jnp.pi / (screening * screening))
    return (kernel * (1.0 / grid**3)).reshape(grid, 16 * grid)


def local(targets, occupied, sphere_map):
    tables = make_tables()
    y, zhi, zlo = lax.axis_index("y"), lax.axis_index("zhi"), lax.axis_index("zlo")
    place = jnp.stack([(y + 4 - zhi) % 4, zlo, (y + 4 - zhi) % 4]).astype(jnp.int32)
    weights = screened_weights((lax.axis_index("x") * 2 + lax.axis_index("core")) * 16)

    def table(name):
        return [jnp.asarray(part) for part in tables[name]]

    def turned(name):
        return [lax.dynamic_index_in_dim(jnp.asarray(part), zhi, 0, keepdims=False) for part in tables[name]]

    band = send(targets.reshape(512, grid), moved(swapped))
    bands = [band] + [send(band, along_y(step)) for step in range(1, 4)]
    blocks = ring(occupied.reshape(512, grid))
    cells = send(sphere_map, moved(swapped)).reshape(1, 4096)
    mask = call(mask_kernel, floats(512, grid), [vmem], cells)

    spread = call(
        density_kernel, floats(8, 4, 4, 32, grid), [smem] + [vmem] * 16,
        place, *bands, *blocks, *table("z"), *table("y"),
    )
    arrived = lax.all_to_all(spread, ("x", "core"), 0, 0, tiled=True)
    back = call(
        convolve_kernel, floats(4096, grid), [vmem] * 6,
        arrived.reshape(4096, grid), weights, *turned("x"), *turned("xi"),
    )
    returned = lax.all_to_all(back.reshape(8, 4, 4, 32, grid), ("x", "core"), 0, 0, tiled=True)
    parts = call(
        field_kernel, [floats(512, grid)] * 4, [smem] + [vmem] * 13,
        place, returned, *blocks, *table("yi"), *table("zi"),
    )
    sums = [parts[0]] + [send(parts[step], along_y(step)) for step in range(1, 4)]
    lines = call(
        applied_kernel, floats(32, 4, 8, grid), [vmem] * 8, *sums, *table("z"), *table("y_end")
    )
    lines = lax.all_to_all(lines, ("x", "y", "core"), 0, 0, tiled=True)
    picked = call(
        pick_kernel, floats(2, 4096), [vmem] * 5,
        lines.reshape(1024, grid), cells, mask, *table("x_end"),
    )
    return send(picked, moved(swapped))[None]


def solution(mesh):
    split = Mesh(mesh.devices.reshape(tuple(extent[a] for a in axes)), axes)
    bands, planes = ("zlo", "y"), ("x", "zhi", "core")
    return jax.shard_map(
        local,
        mesh=split,
        in_specs=(P(bands, planes, None, None), P(bands, planes, None, None), P(planes)),
        out_specs=P(bands, None, planes),
        check_vma=False,
    )
```

```python
import functools

import jax
import jax.numpy as jnp
import ml_dtypes
import numpy as np
from jax import lax
from jax.experimental import pallas as pl
from jax.experimental.pallas import tpu as pltpu
from jax.sharding import Mesh
from jax.sharding import PartitionSpec as P

box_length = 82.0
screening = 0.106
grid = 128
axes = ("zlo", "y", "x", "zhi", "core")
extent = {"zlo": 2, "y": 4, "x": 4, "zhi": 4, "core": 2}
vmem = pl.BlockSpec(memory_space=pltpu.VMEM)
smem = pl.BlockSpec(memory_space=pltpu.SMEM)
params = pltpu.CompilerParams(vmem_limit_bytes=16 * 1024 * 1024)


def split_table(table):
    high = table.astype(ml_dtypes.bfloat16)
    low = (table - high.astype(np.float64)).astype(ml_dtypes.bfloat16)
    return high, low


def waves(rows, cols):
    angles = (np.outer(rows, cols) % grid) * (2.0 * np.pi / grid)
    return np.cos(angles), np.sin(angles)


def base_table():
    cosine, sine = waves(np.arange(grid), np.arange(grid))
    return np.stack(split_table(np.block([[cosine, sine], [-sine, cosine]])))


names = ("z", "zi", "y", "yi", "x", "xi", "y_end", "x_end")
steps = tuple((r, c) for r in (2, 1, 3, 0) for c in (0, 1))
returns = (2, 1, 3, 0)
parts = ((0, 3), (3, 1))


def halves(value):
    high = value.astype(jnp.bfloat16)
    low = (value - high.astype(jnp.float32)).astype(jnp.bfloat16)
    return high, low


def product(left, right):
    def one(a, b):
        return lax.dot_general(a, b, (((1,), (0,)), ((), ())), preferred_element_type=jnp.float32)

    return one(left[0], right[0]) + (one(left[0], right[1]) + one(left[1], right[0]))


def read(pair):
    return pair[0], pair[1]


def planes_to_columns(value):
    top = [value[p * grid : (p + 1) * grid, :grid] for p in range(4)]
    low = [value[p * grid : (p + 1) * grid, grid:] for p in range(4)]
    return jnp.concatenate([jnp.concatenate(top, axis=1), jnp.concatenate(low, axis=1)], axis=0)


def columns_to_planes(value):
    parts = []
    for p in range(4):
        block = value[:, p * grid : (p + 1) * grid]
        parts.append(jnp.concatenate([block[:grid], block[grid:]], axis=1))
    return jnp.concatenate(parts, axis=0)


def choose(index, refs):
    value = refs[0][...]
    for at in range(1, len(refs)):
        value = jnp.where(index == at, refs[at][...], value)
    return value


def part(ref, at, rows):
    return ref[pl.ds(at * rows, rows), :]


def table_kernel(place, base, *outs):
    x, core, y, zhi, side = (place[8 + n] for n in range(5))
    at = lax.broadcasted_iota(jnp.int32, (2 * grid, 1), 0)
    goal = lax.broadcasted_iota(jnp.int32, (2 * grid, 2 * grid), 1)

    def pick(index, values):
        out = values[0]
        for n in range(1, len(values)):
            out = jnp.where(index == n, values[n], out)
        return out

    def order(index):
        return (goal == index).astype(jnp.bfloat16)

    step = at >> 5
    far = pick(step >> 1, (2, 1, 3, 0))
    twin = (core + step) & 1

    def block(sign):
        chip = ((x + 4 + sign * far) & 3) * 2 + twin
        return ((at >> 4) & 1) * grid + chip * 16 + (at & 15)

    def planes(sign, piece):
        line = (sign * 32 * far + grid + 8 * piece + 4 * twin + ((at >> 1) & 3)) & (grid - 1)
        return (at & 1) * grid + line

    slot = (at >> 3) & 3
    staged = (zhi + 4 + pick(slot, (0, side, -side, 2))) & 3
    returned = (y + 2 + pick(slot, returns)) & 3
    line = ((at >> 6) & 3) * 32 + (((at >> 4) + 3 + side) & 3) * 8 + ((at >> 3) & 1) * 4
    row_end = ((at >> 2) & 1) * grid + line + (at & 3)
    column_end = (at & 1) * grid + line + ((at >> 1) & 3)

    def turned(left, right):
        product = lax.dot_general(
            left, right, (((1,), (1,)), ((), ())), preferred_element_type=jnp.float32
        )
        return product.astype(jnp.bfloat16)

    same = order(at)
    rows_y, columns_y = order(block(1)), order(block(-1))
    columns_x, rows_x = order(planes(-1, staged)), order(planes(1, returned))
    rows_end, columns_end = order(row_end), order(column_end)
    for half in range(2):
        forward = base[half]
        inverse = turned(same, forward)
        values = (
            inverse,
            forward,
            turned(rows_y, inverse),
            turned(inverse, columns_y),
            turned(forward, columns_x),
            turned(rows_x, forward),
            turned(rows_end, inverse),
            turned(forward, columns_end),
        )
        for out, value in zip(outs, values):
            out[half] = value


def density_kernel(place, *refs):
    targets, pairs, z_table, y_table, outs = refs[:4], refs[4:12], read(refs[12]), read(refs[13]), refs[14:]
    for at in range(4):
        band = choose(place[at], targets)
        packed = jnp.concatenate([band * pairs[2 * at][...], band * pairs[2 * at + 1][...]], axis=1)
        lines = product(halves(packed), z_table)
        spread = product(y_table, halves(planes_to_columns(lines)))
        for step, out in enumerate(outs):
            for p in range(4):
                out[pl.ds((at * 4 + p) * 32, 32), :] = spread[
                    step * 32 : (step + 1) * 32, p * grid : (p + 1) * grid
                ]


def convolve_kernel(weights, x_pair, xi_pair, *refs):
    arrived, outs = refs[:8], refs[8:]
    x_table, xi_table = read(x_pair), read(xi_pair)
    for pair in range(8):
        columns = [
            jnp.concatenate([ref[pl.ds(2 * pair + k, 32, 16), :] for ref in arrived], axis=0)
            for k in range(2)
        ]
        spectrum = product(x_table, halves(jnp.concatenate(columns, axis=1)))
        weight = weights[:, pl.ds(pair * 2 * grid, 2 * grid)]
        scaled = jnp.concatenate([spectrum[:grid] * weight, spectrum[grid:] * weight], axis=0)
        back = product(xi_table, halves(scaled))
        for k in range(2):
            for at, out in enumerate(outs):
                out[pl.ds(2 * pair + k, 32, 16), :] = back[
                    at * 32 : (at + 1) * 32, k * grid : (k + 1) * grid
                ]


def field_kernel(first, place, *refs):
    arrived, owns, others = refs[:8], refs[8:12], refs[12:16]
    yi_table, zi_table, outs = read(refs[16]), read(refs[17]), refs[18:]
    for at, out in enumerate(outs):
        rows = jnp.concatenate(
            [
                jnp.concatenate([part(ref, (first + at) * 4 + p, 32) for ref in arrived], axis=0)
                for p in range(4)
            ],
            axis=1,
        )
        lines = product(yi_table, halves(rows))
        values = product(halves(columns_to_planes(lines)), zi_table)
        own, other = choose(place[4 + first + at], owns), choose(place[4 + first + at], others)
        out[...] = -(own * values[:, :grid] + other * values[:, grid:])


def applied_kernel(own, one, two, three, z_pair, y_pair, out):
    applied = (own[...] + one[...]) + (two[...] + three[...])
    lines = product(halves(applied), (z_pair[0, :grid], z_pair[1, :grid]))
    spread = product(read(y_pair), halves(planes_to_columns(lines)))
    for p in range(4):
        out[:, pl.ds(p, 1)] = spread[:, p * grid : (p + 1) * grid].reshape(32, 1, 8, grid)


def mask_kernel(cells, out):
    cell = cells[...]
    rows = cell // grid
    row_hot = (lax.broadcasted_iota(jnp.int32, (512, 4096), 0) == rows).astype(jnp.bfloat16)
    lane_hot = (lax.broadcasted_iota(jnp.int32, (grid, 4096), 0) == cell % grid).astype(jnp.bfloat16)
    out[...] = lax.dot_general(
        row_hot, lane_hot, (((1,), (1,)), ((), ())), preferred_element_type=jnp.float32
    )


def pick_kernel(arrived, cells, mask, x_pair, out):
    x_table = read(x_pair)
    lane = lax.broadcasted_iota(jnp.int32, (grid, grid), 0)
    group = lax.broadcasted_iota(jnp.int32, (grid, grid), 1)
    total = jnp.zeros((2 * grid, grid), jnp.float32)
    for pair in range(2):
        columns = [arrived[pl.ds(2 * pair + k, 2 * grid, 4), :] for k in range(2)]
        spectrum = product(x_table, halves(jnp.concatenate(columns, axis=1)))
        for k in range(2):
            row = 2 * pair + k
            kept = mask[pl.ds(row, grid, 4), :]
            part = spectrum[:, k * grid : (k + 1) * grid]
            part = jnp.concatenate([part[:grid] * kept, part[grid:] * kept], axis=0)
            ones = (group == row * 8 + lane // 16).astype(jnp.bfloat16)
            for piece in halves(part):
                total = total + lax.dot_general(
                    piece, ones, (((1,), (0,)), ((), ())), preferred_element_type=jnp.float32
                )
    cell = cells[...]
    plane_hot = (lax.broadcasted_iota(jnp.int32, (grid, 4096), 0) == cell // 512).astype(jnp.bfloat16)
    run_hot = lax.broadcasted_iota(jnp.int32, (32, 4096), 0) == (cell // 16) % 32
    norm = 1.0 / float(np.sqrt(float(grid) ** 3))
    for c in range(2):
        runs = total[c * grid : (c + 1) * grid].T[:32]
        spread = jnp.zeros((32, 4096), jnp.float32)
        for piece in halves(runs):
            spread = spread + lax.dot_general(
                piece, plane_hot, (((1,), (0,)), ((), ())), preferred_element_type=jnp.float32
            )
        out[pl.ds(c, 1), :] = (
            jnp.sum(jnp.where(run_hot, spread, 0.0), axis=0, keepdims=True) * norm
        )


def call(kernel, shapes, specs, *args, flops=1 << 30):
    return pl.pallas_call(
        kernel,
        out_shape=shapes,
        in_specs=specs,
        out_specs=jax.tree.map(lambda _: vmem, shapes),
        compiler_params=params,
        cost_estimate=pl.CostEstimate(flops=flops, bytes_accessed=1 << 20, transcendentals=0),
    )(*args)


def floats(*shape):
    return jax.ShapeDtypeStruct(shape, jnp.float32)


def moved(change):
    pairs = []
    sizes = tuple(extent[a] for a in axes)
    for at in np.ndindex(sizes):
        spot = dict(zip(axes, at))
        goal = change(dict(spot))
        pairs.append((int(np.ravel_multi_index(at, sizes)),
                      int(np.ravel_multi_index(tuple(goal[a] for a in axes), sizes))))
    return pairs


def swapped(spot):
    turn = 2 * spot["zlo"]
    spot["y"], spot["zhi"] = (spot["zhi"] + 2 + turn) % 4, (spot["y"] + turn) % 4
    return spot


def swapped_back(spot):
    turn = 2 * spot["zlo"]
    spot["y"], spot["zhi"] = (spot["zhi"] + turn) % 4, (spot["y"] + 2 + turn) % 4
    return spot


def along_y(step):
    def change(spot):
        spot["y"] = (spot["y"] + step) % 4
        return spot

    return moved(change)


def along_x(step, turn):
    def change(spot):
        spot["x"] = (spot["x"] + step) % 4
        spot["core"] = (spot["core"] + turn) % 2
        return spot

    return moved(change)


def with_partner(spot):
    spot["zlo"] = 1 - spot["zlo"]
    return spot


def with_border(spot):
    z = (spot["zhi"] * 2 + spot["zlo"] + (1 if spot["zlo"] else -1)) % 8
    spot["zhi"], spot["zlo"] = z // 2, z % 2
    return spot


def send(value, pairs):
    return lax.ppermute(value, axes, pairs)


def after(value, *others):
    return lax.optimization_barrier((value,) + others)[0]


def screened_weights(first_row):
    counter = jnp.arange(grid, dtype=jnp.int32)
    folded = jnp.where(counter < grid // 2, counter, counter - grid).astype(jnp.float32)
    rows = first_row + jnp.arange(16, dtype=jnp.int32)
    folded_rows = jnp.where(rows < grid // 2, rows, rows - grid).astype(jnp.float32)
    factor = (2.0 * jnp.pi / box_length) ** 2
    square_norm = factor * (
        folded[:, None, None] ** 2 + folded_rows[None, :, None] ** 2 + folded[None, None, :] ** 2
    )
    safe_square = jnp.where(square_norm > 0, square_norm, 1.0)
    screened = 4.0 * jnp.pi / safe_square * (1.0 - jnp.exp(-safe_square / (4.0 * screening * screening)))
    kernel = jnp.where(square_norm > 0, screened, jnp.pi / (screening * screening))
    return (kernel * (1.0 / grid**3)).reshape(grid, 16 * grid)


def exchange(blocks):
    return [
        block if step == (0, 0) else send(block, along_x(*step)) for step, block in zip(steps, blocks)
    ]


def local(targets, occupied, sphere_map):
    spot = {name: lax.axis_index(name) for name in axes}
    x, y, zhi, zlo, core = (spot[name] for name in ("x", "y", "zhi", "zlo", "core"))
    side = 2 * zlo - 1
    chip = x * 2 + core
    turns = (0, side, -side, 2)
    turned = (y + 2 * zlo) % 4
    band_at = [(turned + 10 - zhi - turn) % 4 for turn in turns]
    ahead = [(turned + k + 6 - zhi) % 4 for k in returns]
    stage_at = [
        jnp.where(m == 0, 0, jnp.where(m == 2, 3, jnp.where(m == (4 + side) % 4, 1, 2))) for m in ahead
    ]
    place = jnp.stack(band_at + stage_at + [x, core, turned, zhi, side]).astype(jnp.int32)

    own = occupied.reshape(512, grid)
    partner, border = moved(with_partner), moved(with_border)
    band = send(targets.reshape(512, grid), moved(swapped))
    a1, b1 = send(own, partner), send(own, border)
    a2, b2 = send(b1, partner), send(a1, border)
    tables = call(
        table_kernel, [jax.ShapeDtypeStruct((2, 2 * grid, 2 * grid), jnp.bfloat16)] * 8,
        [smem, vmem], place, jnp.asarray(base_table()),
    )
    weights = screened_weights(chip * 16)
    a2, b2, weights, tables = lax.optimization_barrier((a2, b2, weights, tables))
    tables = dict(zip(names, tables))
    bands = [band] + [None] * 3
    for step in (2, 1, 3):
        bands[step] = send(band, along_y(step))
    a3, b3 = send(b2, partner), send(a2, border)
    a3, b3, bands = lax.optimization_barrier((a3, b3, bands))
    c4 = jnp.concatenate([send(b3[:256], partner), send(a3[256:], border)])
    owns, others = [own, b2, a2, c4], [a1, b1, a3, b3]

    pairs = [ref for stage in range(4) for ref in (owns[stage], others[stage])]
    blocks = call(
        density_kernel, [floats(512, grid)] * 8, [smem] + [vmem] * 14,
        place, *bands, *pairs, tables["z"], tables["y"],
    )
    arrived = exchange(blocks)
    back = call(
        convolve_kernel, [floats(512, grid)] * 8, [vmem] * 11,
        weights, tables["x"], tables["xi"], *arrived,
    )
    returned = exchange(back)
    sums = {}
    for first, count in parts:
        fields = call(
            functools.partial(field_kernel, first), [floats(512, grid)] * count, [smem] + [vmem] * 18,
            place, *returned, *owns, *others, tables["yi"], tables["zi"],
        )
        for k, field in zip(returns[first:], fields):
            sums[k] = send(field, along_y(k)) if k else field
    cells = send(after(sphere_map, sums[0]), moved(swapped)).reshape(1, 4096)
    mask = call(mask_kernel, floats(512, grid), [vmem], cells)
    sums[0], cells, mask = lax.optimization_barrier((sums[0], cells, mask))
    lines = call(
        applied_kernel, floats(32, 4, 8, grid), [vmem] * 6,
        *[sums[k] for k in range(4)], tables["z"], tables["y_end"],
    )
    lines = lax.all_to_all(lines, ("x", "y", "core"), 0, 0, tiled=True)
    picked = call(
        pick_kernel, floats(2, 4096), [vmem] * 4,
        lines.reshape(1024, grid), cells, mask, tables["x_end"],
    )
    return send(picked, moved(swapped_back))[None]


def solution(mesh):
    split = Mesh(mesh.devices.reshape(tuple(extent[a] for a in axes)), axes)
    bands, planes = ("zlo", "y"), ("x", "zhi", "core")
    return jax.shard_map(
        local,
        mesh=split,
        in_specs=(P(bands, planes, None, None), P(bands, planes, None, None), P(planes)),
        out_specs=P(bands, None, planes),
        check_vma=False,
    )
```

```python
import functools

import jax
import jax.numpy as jnp
import ml_dtypes
import numpy as np
from jax import lax
from jax.experimental import pallas as pl
from jax.experimental.pallas import tpu as pltpu
from jax.sharding import Mesh
from jax.sharding import PartitionSpec as P

box_length = 82.0
screening = 0.106
grid = 128
axes = ("zlo", "y", "x", "zhi", "core")
extent = {"zlo": 2, "y": 4, "x": 4, "zhi": 4, "core": 2}
vmem = pl.BlockSpec(memory_space=pltpu.VMEM)
smem = pl.BlockSpec(memory_space=pltpu.SMEM)
params = pltpu.CompilerParams(vmem_limit_bytes=16 * 1024 * 1024)


def split_table(table):
    high = table.astype(ml_dtypes.bfloat16)
    low = (table - high.astype(np.float64)).astype(ml_dtypes.bfloat16)
    return high, low


def waves(rows, cols):
    angles = (np.outer(rows, cols) % grid) * (2.0 * np.pi / grid)
    return np.cos(angles), np.sin(angles)


def base_table():
    cosine, sine = waves(np.arange(grid), np.arange(grid))
    return np.stack(split_table(np.block([[cosine, sine], [-sine, cosine]])))


names = ("z", "zi", "y", "yi", "x", "xi", "y_end", "x_end")
steps = tuple((r, c) for r in (2, 1, 3, 0) for c in (0, 1))
returns = (2, 1, 3, 0)
parts = ((0, 3), (3, 1))


def halves(value):
    high = value.astype(jnp.bfloat16)
    low = (value - high.astype(jnp.float32)).astype(jnp.bfloat16)
    return high, low


def product(left, right):
    def one(a, b):
        return lax.dot_general(a, b, (((1,), (0,)), ((), ())), preferred_element_type=jnp.float32)

    return one(left[0], right[0]) + (one(left[0], right[1]) + one(left[1], right[0]))


def read(pair):
    return pair[0], pair[1]


def planes_to_columns(value):
    top = [value[p * grid : (p + 1) * grid, :grid] for p in range(4)]
    low = [value[p * grid : (p + 1) * grid, grid:] for p in range(4)]
    return jnp.concatenate([jnp.concatenate(top, axis=1), jnp.concatenate(low, axis=1)], axis=0)


def columns_to_planes(value):
    parts = []
    for p in range(4):
        block = value[:, p * grid : (p + 1) * grid]
        parts.append(jnp.concatenate([block[:grid], block[grid:]], axis=1))
    return jnp.concatenate(parts, axis=0)


def choose(index, refs):
    value = refs[0][...]
    for at in range(1, len(refs)):
        value = jnp.where(index == at, refs[at][...], value)
    return value


def part(ref, at, rows):
    return ref[pl.ds(at * rows, rows), :]


def table_kernel(place, base, *outs):
    x, core, y, zhi, side = (place[8 + n] for n in range(5))
    at = lax.broadcasted_iota(jnp.int32, (2 * grid, 1), 0)
    goal = lax.broadcasted_iota(jnp.int32, (2 * grid, 2 * grid), 1)

    def pick(index, values):
        out = values[0]
        for n in range(1, len(values)):
            out = jnp.where(index == n, values[n], out)
        return out

    def order(index):
        return (goal == index).astype(jnp.bfloat16)

    step = at >> 5
    far = pick(step >> 1, (2, 1, 3, 0))
    twin = (core + step) & 1

    def block(sign):
        chip = ((x + 4 + sign * far) & 3) * 2 + twin
        return ((at >> 4) & 1) * grid + chip * 16 + (at & 15)

    def planes(sign, piece):
        line = (sign * 32 * far + grid + 8 * piece + 4 * twin + ((at >> 1) & 3)) & (grid - 1)
        return (at & 1) * grid + line

    slot = (at >> 3) & 3
    staged = (zhi + 4 + pick(slot, (0, side, -side, 2))) & 3
    returned = (y + 2 + pick(slot, returns)) & 3
    line = ((at >> 6) & 3) * 32 + (((at >> 4) + 3 + side) & 3) * 8 + ((at >> 3) & 1) * 4
    row_end = ((at >> 2) & 1) * grid + line + (at & 3)
    column_end = (at & 1) * grid + line + ((at >> 1) & 3)

    def turned(left, right):
        product = lax.dot_general(
            left, right, (((1,), (1,)), ((), ())), preferred_element_type=jnp.float32
        )
        return product.astype(jnp.bfloat16)

    same = order(at)
    rows_y, columns_y = order(block(1)), order(block(-1))
    columns_x, rows_x = order(planes(-1, staged)), order(planes(1, returned))
    rows_end, columns_end = order(row_end), order(column_end)
    for half in range(2):
        forward = base[half]
        inverse = turned(same, forward)
        values = (
            inverse,
            forward,
            turned(rows_y, inverse),
            turned(inverse, columns_y),
            turned(forward, columns_x),
            turned(rows_x, forward),
            turned(rows_end, inverse),
            turned(forward, columns_end),
        )
        for out, value in zip(outs, values):
            out[half] = value


def density_kernel(first, count, place, *refs):
    targets, pairs, tables = refs[:4], refs[4 : 4 + 2 * count], refs[4 + 2 * count : 6 + 2 * count]
    kept, outs = refs[6 + 2 * count : -8], refs[-8:]
    z_table, y_table = read(tables[0]), read(tables[1])
    for earlier, out in zip(kept, outs):
        out[pl.ds(0, first * 128), :] = earlier[...]
    for at in range(count):
        band = choose(place[first + at], targets)
        packed = jnp.concatenate([band * pairs[2 * at][...], band * pairs[2 * at + 1][...]], axis=1)
        lines = product(halves(packed), z_table)
        spread = product(y_table, halves(planes_to_columns(lines)))
        for step, out in enumerate(outs):
            for p in range(4):
                out[pl.ds(((first + at) * 4 + p) * 32, 32), :] = spread[
                    step * 32 : (step + 1) * 32, p * grid : (p + 1) * grid
                ]


def convolve_kernel(weights, x_pair, xi_pair, *refs):
    arrived, outs = refs[:8], refs[8:]
    x_table, xi_table = read(x_pair), read(xi_pair)
    for pair in range(8):
        columns = [
            jnp.concatenate([ref[pl.ds(2 * pair + k, 32, 16), :] for ref in arrived], axis=0)
            for k in range(2)
        ]
        spectrum = product(x_table, halves(jnp.concatenate(columns, axis=1)))
        weight = weights[:, pl.ds(pair * 2 * grid, 2 * grid)]
        scaled = jnp.concatenate([spectrum[:grid] * weight, spectrum[grid:] * weight], axis=0)
        back = product(xi_table, halves(scaled))
        for k in range(2):
            for at, out in enumerate(outs):
                out[pl.ds(2 * pair + k, 32, 16), :] = back[
                    at * 32 : (at + 1) * 32, k * grid : (k + 1) * grid
                ]


def field_kernel(first, place, *refs):
    arrived, owns, others = refs[:8], refs[8:12], refs[12:16]
    yi_table, zi_table, outs = read(refs[16]), read(refs[17]), refs[18:]
    for at, out in enumerate(outs):
        rows = jnp.concatenate(
            [
                jnp.concatenate([part(ref, (first + at) * 4 + p, 32) for ref in arrived], axis=0)
                for p in range(4)
            ],
            axis=1,
        )
        lines = product(yi_table, halves(rows))
        values = product(halves(columns_to_planes(lines)), zi_table)
        own, other = choose(place[4 + first + at], owns), choose(place[4 + first + at], others)
        out[...] = -(own * values[:, :grid] + other * values[:, grid:])


def applied_kernel(own, one, two, three, z_pair, y_pair, out):
    applied = (own[...] + one[...]) + (two[...] + three[...])
    lines = product(halves(applied), (z_pair[0, :grid], z_pair[1, :grid]))
    spread = product(read(y_pair), halves(planes_to_columns(lines)))
    for p in range(4):
        out[:, pl.ds(p, 1)] = spread[:, p * grid : (p + 1) * grid].reshape(32, 1, 8, grid)


def mask_kernel(cells, out, plane_out, run_out):
    cell = cells[...]

    def hot(count, index):
        return lax.broadcasted_iota(jnp.int32, (count, 4096), 0) == index

    row_hot = hot(512, cell // grid).astype(jnp.bfloat16)
    lane_hot = hot(grid, cell % grid).astype(jnp.bfloat16)
    out[...] = lax.dot_general(
        row_hot, lane_hot, (((1,), (1,)), ((), ())), preferred_element_type=jnp.float32
    )
    plane_out[...] = hot(grid, cell // 512).astype(jnp.bfloat16)
    run_out[...] = hot(32, (cell // 16) % 32).astype(jnp.float32)


def pick_kernel(arrived, mask, planes, runs_at, x_pair, out):
    x_table = read(x_pair)
    lane = lax.broadcasted_iota(jnp.int32, (grid, grid), 0)
    group = lax.broadcasted_iota(jnp.int32, (grid, grid), 1)
    total = jnp.zeros((2 * grid, grid), jnp.float32)
    for pair in range(2):
        columns = [arrived[pl.ds(2 * pair + k, 2 * grid, 4), :] for k in range(2)]
        spectrum = product(x_table, halves(jnp.concatenate(columns, axis=1)))
        for k in range(2):
            row = 2 * pair + k
            kept = mask[pl.ds(row, grid, 4), :]
            part = spectrum[:, k * grid : (k + 1) * grid]
            part = jnp.concatenate([part[:grid] * kept, part[grid:] * kept], axis=0)
            ones = (group == row * 8 + lane // 16).astype(jnp.bfloat16)
            for piece in halves(part):
                total = total + lax.dot_general(
                    piece, ones, (((1,), (0,)), ((), ())), preferred_element_type=jnp.float32
                )
    norm = 1.0 / float(np.sqrt(float(grid) ** 3))
    for c in range(2):
        runs = total[c * grid : (c + 1) * grid].T[:32]
        spread = jnp.zeros((32, 4096), jnp.float32)
        for piece in halves(runs):
            spread = spread + lax.dot_general(
                piece, planes[...], (((1,), (0,)), ((), ())), preferred_element_type=jnp.float32
            )
        out[pl.ds(c, 1), :] = (
            jnp.sum(runs_at[...] * spread, axis=0, keepdims=True) * norm
        )


def call(kernel, shapes, specs, *args, flops=1 << 30):
    return pl.pallas_call(
        kernel,
        out_shape=shapes,
        in_specs=specs,
        out_specs=jax.tree.map(lambda _: vmem, shapes),
        compiler_params=params,
        cost_estimate=pl.CostEstimate(flops=flops, bytes_accessed=1 << 20, transcendentals=0),
    )(*args)


def floats(*shape):
    return jax.ShapeDtypeStruct(shape, jnp.float32)


def moved(change):
    pairs = []
    sizes = tuple(extent[a] for a in axes)
    for at in np.ndindex(sizes):
        spot = dict(zip(axes, at))
        goal = change(dict(spot))
        pairs.append((int(np.ravel_multi_index(at, sizes)),
                      int(np.ravel_multi_index(tuple(goal[a] for a in axes), sizes))))
    return pairs


def swapped(spot):
    turn = 2 * spot["zlo"]
    spot["y"], spot["zhi"] = (spot["zhi"] + 2 + turn) % 4, (spot["y"] + turn) % 4
    return spot


def swapped_back(spot):
    turn = 2 * spot["zlo"]
    spot["y"], spot["zhi"] = (spot["zhi"] + turn) % 4, (spot["y"] + 2 + turn) % 4
    return spot


def along_y(step):
    def change(spot):
        spot["y"] = (spot["y"] + step) % 4
        return spot

    return moved(change)


def along_x(step, turn):
    def change(spot):
        spot["x"] = (spot["x"] + step) % 4
        spot["core"] = (spot["core"] + turn) % 2
        return spot

    return moved(change)


def with_partner(spot):
    spot["zlo"] = 1 - spot["zlo"]
    return spot


def with_border(spot):
    z = (spot["zhi"] * 2 + spot["zlo"] + (1 if spot["zlo"] else -1)) % 8
    spot["zhi"], spot["zlo"] = z // 2, z % 2
    return spot


def send(value, pairs):
    return lax.ppermute(value, axes, pairs)


def after(value, *others):
    return lax.optimization_barrier((value,) + others)[0]


def screened_weights(first_row):
    counter = jnp.arange(grid, dtype=jnp.int32)
    folded = jnp.where(counter < grid // 2, counter, counter - grid).astype(jnp.float32)
    rows = first_row + jnp.arange(16, dtype=jnp.int32)
    folded_rows = jnp.where(rows < grid // 2, rows, rows - grid).astype(jnp.float32)
    factor = (2.0 * jnp.pi / box_length) ** 2
    square_norm = factor * (
        folded[:, None, None] ** 2 + folded_rows[None, :, None] ** 2 + folded[None, None, :] ** 2
    )
    safe_square = jnp.where(square_norm > 0, square_norm, 1.0)
    screened = 4.0 * jnp.pi / safe_square * (1.0 - jnp.exp(-safe_square / (4.0 * screening * screening)))
    kernel = jnp.where(square_norm > 0, screened, jnp.pi / (screening * screening))
    return (kernel * (1.0 / grid**3)).reshape(grid, 16 * grid)


def exchange(blocks):
    return [
        block if step == (0, 0) else send(block, along_x(*step)) for step, block in zip(steps, blocks)
    ]


def local(targets, occupied, sphere_map):
    spot = {name: lax.axis_index(name) for name in axes}
    x, y, zhi, zlo, core = (spot[name] for name in ("x", "y", "zhi", "zlo", "core"))
    side = 2 * zlo - 1
    chip = x * 2 + core
    turns = (0, side, -side, 2)
    turned = (y + 2 * zlo) % 4
    band_at = [(turned + 10 - zhi - turn) % 4 for turn in turns]
    ahead = [(turned + k + 6 - zhi) % 4 for k in returns]
    stage_at = [
        jnp.where(m == 0, 0, jnp.where(m == 2, 3, jnp.where(m == (4 + side) % 4, 1, 2))) for m in ahead
    ]
    place = jnp.stack(band_at + stage_at + [x, core, turned, zhi, side]).astype(jnp.int32)

    own = occupied.reshape(512, grid)
    partner, border = moved(with_partner), moved(with_border)
    band = send(targets.reshape(512, grid), moved(swapped))
    a1, b1 = send(own, partner), send(own, border)
    tables = call(
        table_kernel, [jax.ShapeDtypeStruct((2, 2 * grid, 2 * grid), jnp.bfloat16)] * 8,
        [smem, vmem], place, jnp.asarray(base_table()),
    )
    weights = screened_weights(chip * 16)
    a1, b1, weights, tables = lax.optimization_barrier((a1, b1, weights, tables))
    a2, b2 = send(b1, partner), send(a1, border)
    tables = dict(zip(names, tables))
    bands = [band] + [None] * 3
    for step in (2, 1, 3):
        bands[step] = send(band, along_y(step))
    a3, b3 = send(b2, partner), send(a2, border)
    a3, b3, bands[2] = lax.optimization_barrier((a3, b3, bands[2]))
    c4 = jnp.concatenate([send(b3[:256], partner), send(a3[256:], border)])
    owns, others = [own, b2, a2, c4], [a1, b1, a3, b3]

    blocks = call(
        functools.partial(density_kernel, 0, 3), [floats(384, grid)] * 8, [smem] + [vmem] * 12,
        place, *bands, own, a1, b2, b1, a2, a3, tables["z"], tables["y"],
    )
    blocks = call(
        functools.partial(density_kernel, 3, 1), [floats(512, grid)] * 8, [smem] + [vmem] * 16,
        place, *bands, c4, b3, tables["z"], tables["y"], *blocks,
    )
    arrived = exchange(blocks)
    back = call(
        convolve_kernel, [floats(512, grid)] * 8, [vmem] * 11,
        weights, tables["x"], tables["xi"], *arrived,
    )
    returned = exchange(back)
    sums = {}
    for first, count in parts:
        fields = call(
            functools.partial(field_kernel, first), [floats(512, grid)] * count, [smem] + [vmem] * 18,
            place, *returned, *owns, *others, tables["yi"], tables["zi"],
        )
        for k, field in zip(returns[first:], fields):
            sums[k] = send(field, along_y(k)) if k else field
    cells = send(after(sphere_map, sums[0]), moved(swapped)).reshape(1, 4096)
    picks = call(
        mask_kernel,
        [floats(512, grid), jax.ShapeDtypeStruct((grid, 4096), jnp.bfloat16), floats(32, 4096)],
        [vmem], cells,
    )
    sums[0], picks = lax.optimization_barrier((sums[0], picks))
    lines = call(
        applied_kernel, floats(32, 4, 8, grid), [vmem] * 6,
        *[sums[k] for k in range(4)], tables["z"], tables["y_end"],
    )
    lines = lax.all_to_all(lines, ("x", "y", "core"), 0, 0, tiled=True)
    picked = call(
        pick_kernel, floats(2, 4096), [vmem] * 5,
        lines.reshape(1024, grid), *picks, tables["x_end"],
    )
    return send(picked, moved(swapped_back))[None]


def solution(mesh):
    split = Mesh(mesh.devices.reshape(tuple(extent[a] for a in axes)), axes)
    bands, planes = ("zlo", "y"), ("x", "zhi", "core")
    return jax.shard_map(
        local,
        mesh=split,
        in_specs=(P(bands, planes, None, None), P(bands, planes, None, None), P(planes)),
        out_specs=P(bands, None, planes),
        check_vma=False,
    )
```

```python
import functools

import jax
import jax.numpy as jnp
import ml_dtypes
import numpy as np
from jax import lax
from jax.experimental import pallas as pl
from jax.experimental.pallas import tpu as pltpu
from jax.sharding import Mesh
from jax.sharding import PartitionSpec as P

box_length = 82.0
screening = 0.106
grid = 128
axes = ("zlo", "y", "x", "zhi", "core")
extent = {"zlo": 2, "y": 4, "x": 4, "zhi": 4, "core": 2}
vmem = pl.BlockSpec(memory_space=pltpu.VMEM)
smem = pl.BlockSpec(memory_space=pltpu.SMEM)
params = pltpu.CompilerParams(vmem_limit_bytes=16 * 1024 * 1024)


def split_table(table):
    high = table.astype(ml_dtypes.bfloat16)
    low = (table - high.astype(np.float64)).astype(ml_dtypes.bfloat16)
    return high, low


def waves(rows, cols):
    angles = (np.outer(rows, cols) % grid) * (2.0 * np.pi / grid)
    return np.cos(angles), np.sin(angles)


def base_table():
    cosine, sine = waves(np.arange(grid), np.arange(grid))
    return np.stack(split_table(np.block([[cosine, sine], [-sine, cosine]])))


names = ("z", "zi", "y", "yi", "x", "xi", "y_end", "x_end")
steps = tuple((r, c) for r in (2, 1, 3, 0) for c in (0, 1))
returns = (2, 1, 3, 0)
parts = ((0, 3), (3, 1))


def halves(value):
    high = value.astype(jnp.bfloat16)
    low = (value - high.astype(jnp.float32)).astype(jnp.bfloat16)
    return high, low


def product(left, right):
    def one(a, b):
        return lax.dot_general(a, b, (((1,), (0,)), ((), ())), preferred_element_type=jnp.float32)

    return one(left[0], right[0]) + (one(left[0], right[1]) + one(left[1], right[0]))


def read(pair):
    return pair[0], pair[1]


def planes_to_columns(value):
    top = [value[p * grid : (p + 1) * grid, :grid] for p in range(4)]
    low = [value[p * grid : (p + 1) * grid, grid:] for p in range(4)]
    return jnp.concatenate([jnp.concatenate(top, axis=1), jnp.concatenate(low, axis=1)], axis=0)


def columns_to_planes(value):
    parts = []
    for p in range(4):
        block = value[:, p * grid : (p + 1) * grid]
        parts.append(jnp.concatenate([block[:grid], block[grid:]], axis=1))
    return jnp.concatenate(parts, axis=0)


def choose(index, refs):
    value = refs[0][...]
    for at in range(1, len(refs)):
        value = jnp.where(index == at, refs[at][...], value)
    return value


def part(ref, at, rows):
    return ref[pl.ds(at * rows, rows), :]


def table_kernel(place, base, *outs):
    x, core, y, zhi, side = (place[8 + n] for n in range(5))
    at = lax.broadcasted_iota(jnp.int32, (2 * grid, 1), 0)
    goal = lax.broadcasted_iota(jnp.int32, (2 * grid, 2 * grid), 1)

    def pick(index, values):
        out = values[0]
        for n in range(1, len(values)):
            out = jnp.where(index == n, values[n], out)
        return out

    def order(index):
        return (goal == index).astype(jnp.bfloat16)

    step = at >> 5
    far = pick(step >> 1, (2, 1, 3, 0))
    twin = (core + step) & 1

    def block(sign):
        chip = ((x + 4 + sign * far) & 3) * 2 + twin
        return ((at >> 4) & 1) * grid + chip * 16 + (at & 15)

    def planes(sign, piece):
        line = (sign * 32 * far + grid + 8 * piece + 4 * twin + ((at >> 1) & 3)) & (grid - 1)
        return (at & 1) * grid + line

    slot = (at >> 3) & 3
    staged = (zhi + 4 + pick(slot, (0, side, -side, 2))) & 3
    returned = (y + 2 + pick(slot, returns)) & 3
    line = ((at >> 6) & 3) * 32 + (((at >> 4) + 3 + side) & 3) * 8 + ((at >> 3) & 1) * 4
    row_end = ((at >> 2) & 1) * grid + line + (at & 3)
    column_end = (at & 1) * grid + line + ((at >> 1) & 3)

    def turned(left, right):
        product = lax.dot_general(
            left, right, (((1,), (1,)), ((), ())), preferred_element_type=jnp.float32
        )
        return product.astype(jnp.bfloat16)

    same = order(at)
    rows_y, columns_y = order(block(1)), order(block(-1))
    columns_x, rows_x = order(planes(-1, staged)), order(planes(1, returned))
    rows_end, columns_end = order(row_end), order(column_end)
    for half in range(2):
        forward = base[half]
        inverse = turned(same, forward)
        values = (
            inverse,
            forward,
            turned(rows_y, inverse),
            turned(inverse, columns_y),
            turned(forward, columns_x),
            turned(rows_x, forward),
            turned(rows_end, inverse),
            turned(forward, columns_end),
        )
        for out, value in zip(outs, values):
            out[half] = value


def whole(ref):
    if isinstance(ref, tuple):
        return jnp.concatenate([half[...] for half in ref], axis=0)
    return ref[...]


def density_kernel(first, count, place, *refs):
    targets, refs = refs[:4], refs[4:]
    if first:
        refs = (refs[:2],) + refs[2:]
    pairs, tables = refs[: 2 * count], refs[2 * count : 2 * count + 2]
    kept, outs = refs[2 * count + 2 : -8], refs[-8:]
    z_table, y_table = read(tables[0]), read(tables[1])
    for at in range(count):
        band = choose(place[first + at], targets)
        packed = jnp.concatenate([band * whole(pairs[2 * at]), band * whole(pairs[2 * at + 1])], axis=1)
        lines = product(halves(packed), z_table)
        spread = product(y_table, halves(planes_to_columns(lines)))
        for step, out in enumerate(outs):
            for p in range(4):
                out[pl.ds(((first + at) * 4 + p) * 32, 32), :] = spread[
                    step * 32 : (step + 1) * 32, p * grid : (p + 1) * grid
                ]
    for earlier, out in zip(kept, outs):
        out[pl.ds(0, first * 128), :] = earlier[...]


def convolve_kernel(weights, x_pair, xi_pair, *refs):
    arrived, outs = refs[:8], refs[8:]
    x_table, xi_table = read(x_pair), read(xi_pair)
    for pair in range(8):
        columns = [
            jnp.concatenate([ref[pl.ds(2 * pair + k, 32, 16), :] for ref in arrived], axis=0)
            for k in range(2)
        ]
        spectrum = product(x_table, halves(jnp.concatenate(columns, axis=1)))
        weight = weights[:, pl.ds(pair * 2 * grid, 2 * grid)]
        scaled = jnp.concatenate([spectrum[:grid] * weight, spectrum[grid:] * weight], axis=0)
        back = product(xi_table, halves(scaled))
        for k in range(2):
            for at, out in enumerate(outs):
                out[pl.ds(2 * pair + k, 32, 16), :] = back[
                    at * 32 : (at + 1) * 32, k * grid : (k + 1) * grid
                ]


def field_kernel(first, place, *refs):
    arrived, owns, others = refs[:8], refs[8:12], refs[12:16]
    yi_table, zi_table, outs = read(refs[16]), read(refs[17]), refs[18:]
    for at, out in enumerate(outs):
        rows = jnp.concatenate(
            [
                jnp.concatenate([part(ref, (first + at) * 4 + p, 32) for ref in arrived], axis=0)
                for p in range(4)
            ],
            axis=1,
        )
        lines = product(yi_table, halves(rows))
        values = product(halves(columns_to_planes(lines)), zi_table)
        own, other = choose(place[4 + first + at], owns), choose(place[4 + first + at], others)
        out[...] = -(own * values[:, :grid] + other * values[:, grid:])


def applied_kernel(own, one, two, three, z_pair, y_pair, out):
    applied = (own[...] + one[...]) + (two[...] + three[...])
    lines = product(halves(applied), (z_pair[0, :grid], z_pair[1, :grid]))
    spread = product(read(y_pair), halves(planes_to_columns(lines)))
    for p in range(4):
        out[:, pl.ds(p, 1)] = spread[:, p * grid : (p + 1) * grid].reshape(32, 1, 8, grid)


def mask_kernel(cells, out, plane_out, run_out):
    cell = cells[...]

    def hot(count, index):
        return lax.broadcasted_iota(jnp.int32, (count, 4096), 0) == index

    row_hot = hot(512, cell // grid).astype(jnp.bfloat16)
    lane_hot = hot(grid, cell % grid).astype(jnp.bfloat16)
    out[...] = lax.dot_general(
        row_hot, lane_hot, (((1,), (1,)), ((), ())), preferred_element_type=jnp.float32
    )
    plane_out[...] = hot(grid, cell // 512).astype(jnp.bfloat16)
    run_out[...] = hot(32, (cell // 16) % 32).astype(jnp.float32)


def pick_kernel(arrived, mask, planes, runs_at, x_pair, out):
    x_table = read(x_pair)
    lane = lax.broadcasted_iota(jnp.int32, (grid, grid), 0)
    group = lax.broadcasted_iota(jnp.int32, (grid, grid), 1)
    total = jnp.zeros((2 * grid, grid), jnp.float32)
    for pair in range(2):
        columns = [arrived[pl.ds(2 * pair + k, 2 * grid, 4), :] for k in range(2)]
        spectrum = product(x_table, halves(jnp.concatenate(columns, axis=1)))
        for k in range(2):
            row = 2 * pair + k
            kept = mask[pl.ds(row, grid, 4), :]
            part = spectrum[:, k * grid : (k + 1) * grid]
            part = jnp.concatenate([part[:grid] * kept, part[grid:] * kept], axis=0)
            ones = (group == row * 8 + lane // 16).astype(jnp.bfloat16)
            for piece in halves(part):
                total = total + lax.dot_general(
                    piece, ones, (((1,), (0,)), ((), ())), preferred_element_type=jnp.float32
                )
    norm = 1.0 / float(np.sqrt(float(grid) ** 3))
    for c in range(2):
        runs = total[c * grid : (c + 1) * grid].T[:32]
        spread = jnp.zeros((32, 4096), jnp.float32)
        for piece in halves(runs):
            spread = spread + lax.dot_general(
                piece, planes[...], (((1,), (0,)), ((), ())), preferred_element_type=jnp.float32
            )
        out[pl.ds(c, 1), :] = (
            jnp.sum(runs_at[...] * spread, axis=0, keepdims=True) * norm
        )


def call(kernel, shapes, specs, *args, flops=1 << 30):
    return pl.pallas_call(
        kernel,
        out_shape=shapes,
        in_specs=specs,
        out_specs=jax.tree.map(lambda _: vmem, shapes),
        compiler_params=params,
        cost_estimate=pl.CostEstimate(flops=flops, bytes_accessed=1 << 20, transcendentals=0),
    )(*args)


def floats(*shape):
    return jax.ShapeDtypeStruct(shape, jnp.float32)


def moved(change):
    pairs = []
    sizes = tuple(extent[a] for a in axes)
    for at in np.ndindex(sizes):
        spot = dict(zip(axes, at))
        goal = change(dict(spot))
        pairs.append((int(np.ravel_multi_index(at, sizes)),
                      int(np.ravel_multi_index(tuple(goal[a] for a in axes), sizes))))
    return pairs


def swapped(spot):
    turn = 2 * spot["zlo"]
    spot["y"], spot["zhi"] = (spot["zhi"] + 2 + turn) % 4, (spot["y"] + turn) % 4
    return spot


def swapped_back(spot):
    turn = 2 * spot["zlo"]
    spot["y"], spot["zhi"] = (spot["zhi"] + turn) % 4, (spot["y"] + 2 + turn) % 4
    return spot


def along_y(step):
    def change(spot):
        spot["y"] = (spot["y"] + step) % 4
        return spot

    return moved(change)


def along_x(step, turn):
    def change(spot):
        spot["x"] = (spot["x"] + step) % 4
        spot["core"] = (spot["core"] + turn) % 2
        return spot

    return moved(change)


def with_partner(spot):
    spot["zlo"] = 1 - spot["zlo"]
    return spot


def with_border(spot):
    z = (spot["zhi"] * 2 + spot["zlo"] + (1 if spot["zlo"] else -1)) % 8
    spot["zhi"], spot["zlo"] = z // 2, z % 2
    return spot


def send(value, pairs):
    return lax.ppermute(value, axes, pairs)


def after(value, *others):
    return lax.optimization_barrier((value,) + others)[0]


def screened_weights(first_row):
    counter = jnp.arange(grid, dtype=jnp.int32)
    folded = jnp.where(counter < grid // 2, counter, counter - grid).astype(jnp.float32)
    rows = first_row + jnp.arange(16, dtype=jnp.int32)
    folded_rows = jnp.where(rows < grid // 2, rows, rows - grid).astype(jnp.float32)
    factor = (2.0 * jnp.pi / box_length) ** 2
    square_norm = factor * (
        folded[:, None, None] ** 2 + folded_rows[None, :, None] ** 2 + folded[None, None, :] ** 2
    )
    safe_square = jnp.where(square_norm > 0, square_norm, 1.0)
    screened = 4.0 * jnp.pi / safe_square * (1.0 - jnp.exp(-safe_square / (4.0 * screening * screening)))
    kernel = jnp.where(square_norm > 0, screened, jnp.pi / (screening * screening))
    return (kernel * (1.0 / grid**3)).reshape(grid, 16 * grid)


def exchange(blocks):
    return [
        block if step == (0, 0) else send(block, along_x(*step)) for step, block in zip(steps, blocks)
    ]


def local(targets, occupied, sphere_map):
    spot = {name: lax.axis_index(name) for name in axes}
    x, y, zhi, zlo, core = (spot[name] for name in ("x", "y", "zhi", "zlo", "core"))
    side = 2 * zlo - 1
    chip = x * 2 + core
    turns = (0, side, -side, 2)
    turned = (y + 2 * zlo) % 4
    band_at = [(turned + 10 - zhi - turn) % 4 for turn in turns]
    ahead = [(turned + k + 6 - zhi) % 4 for k in returns]
    stage_at = [
        jnp.where(m == 0, 0, jnp.where(m == 2, 3, jnp.where(m == (4 + side) % 4, 1, 2))) for m in ahead
    ]
    place = jnp.stack(band_at + stage_at + [x, core, turned, zhi, side]).astype(jnp.int32)

    own = occupied.reshape(512, grid)
    partner, border = moved(with_partner), moved(with_border)
    band = send(targets.reshape(512, grid), moved(swapped))
    a1, b1 = send(own, partner), send(own, border)
    tables = call(
        table_kernel, [jax.ShapeDtypeStruct((2, 2 * grid, 2 * grid), jnp.bfloat16)] * 8,
        [smem, vmem], place, jnp.asarray(base_table()),
    )
    weights = screened_weights(chip * 16)
    a1, b1, weights, tables = lax.optimization_barrier((a1, b1, weights, tables))
    a2, b2 = send(b1, partner), send(a1, border)
    tables = dict(zip(names, tables))
    bands = [band] + [None] * 3
    for step in (2, 1, 3):
        bands[step] = send(band, along_y(step))
    a3, b3 = send(b2, partner), send(a2, border)
    a3, b3, bands[2] = lax.optimization_barrier((a3, b3, bands[2]))
    far = [send(b3[:256], partner), send(a3[256:], border)]
    c4 = jnp.concatenate(far)
    owns, others = [own, b2, a2, c4], [a1, b1, a3, b3]

    blocks = call(
        functools.partial(density_kernel, 0, 3), [floats(384, grid)] * 8, [smem] + [vmem] * 12,
        place, *bands, own, a1, b2, b1, a2, a3, tables["z"], tables["y"],
    )
    blocks = call(
        functools.partial(density_kernel, 3, 1), [floats(512, grid)] * 8, [smem] + [vmem] * 17,
        place, *bands, *far, b3, tables["z"], tables["y"], *blocks,
    )
    arrived = exchange(blocks)
    back = call(
        convolve_kernel, [floats(512, grid)] * 8, [vmem] * 11,
        weights, tables["x"], tables["xi"], *arrived,
    )
    returned = exchange(back)
    sums = {}
    for first, count in parts:
        fields = call(
            functools.partial(field_kernel, first), [floats(512, grid)] * count, [smem] + [vmem] * 18,
            place, *returned, *owns, *others, tables["yi"], tables["zi"],
        )
        for k, field in zip(returns[first:], fields):
            sums[k] = send(field, along_y(k)) if k else field
    cells = send(after(sphere_map, sums[0]), moved(swapped)).reshape(1, 4096)
    picks = call(
        mask_kernel,
        [floats(512, grid), jax.ShapeDtypeStruct((grid, 4096), jnp.bfloat16), floats(32, 4096)],
        [vmem], cells,
    )
    sums[0], picks = lax.optimization_barrier((sums[0], picks))
    lines = call(
        applied_kernel, floats(32, 4, 8, grid), [vmem] * 6,
        *[sums[k] for k in range(4)], tables["z"], tables["y_end"],
    )
    lines = lax.all_to_all(lines, ("x", "y", "core"), 0, 0, tiled=True)
    picked = call(
        pick_kernel, floats(2, 4096), [vmem] * 5,
        lines.reshape(1024, grid), *picks, tables["x_end"],
    )
    return send(picked, moved(swapped_back))[None]


def solution(mesh):
    split = Mesh(mesh.devices.reshape(tuple(extent[a] for a in axes)), axes)
    bands, planes = ("zlo", "y"), ("x", "zhi", "core")
    return jax.shard_map(
        local,
        mesh=split,
        in_specs=(P(bands, planes, None, None), P(bands, planes, None, None), P(planes)),
        out_specs=P(bands, None, planes),
        check_vma=False,
    )
```

```python
import functools

import jax
import jax.numpy as jnp
import ml_dtypes
import numpy as np
from jax import lax
from jax.experimental import pallas as pl
from jax.experimental.pallas import tpu as pltpu
from jax.sharding import Mesh
from jax.sharding import PartitionSpec as P

box_length = 82.0
screening = 0.106
grid = 128
axes = ("zlo", "y", "x", "zhi", "core")
extent = {"zlo": 2, "y": 4, "x": 4, "zhi": 4, "core": 2}
vmem = pl.BlockSpec(memory_space=pltpu.VMEM)
smem = pl.BlockSpec(memory_space=pltpu.SMEM)
params = pltpu.CompilerParams(vmem_limit_bytes=16 * 1024 * 1024)


def split_table(table):
    high = table.astype(ml_dtypes.bfloat16)
    low = (table - high.astype(np.float64)).astype(ml_dtypes.bfloat16)
    return high, low


def waves(rows, cols):
    angles = (np.outer(rows, cols) % grid) * (2.0 * np.pi / grid)
    return np.cos(angles), np.sin(angles)


def base_table():
    cosine, sine = waves(np.arange(grid), np.arange(grid))
    return np.stack(split_table(np.block([[cosine, sine], [-sine, cosine]])))


names = ("z", "zi", "y", "yi", "x", "xi", "y_end", "x_end")
steps = ((2, 0), (2, 1), (1, 0), (3, 0), (1, 1), (3, 1), (0, 0), (0, 1))
returns = (2, 1, 3, 0)
parts = ((0, 3), (3, 1))


def halves(value):
    high = value.astype(jnp.bfloat16)
    low = (value - high.astype(jnp.float32)).astype(jnp.bfloat16)
    return high, low


def product(left, right):
    def one(a, b):
        return lax.dot_general(a, b, (((1,), (0,)), ((), ())), preferred_element_type=jnp.float32)

    return one(left[0], right[0]) + (one(left[0], right[1]) + one(left[1], right[0]))


def read(pair):
    return pair[0], pair[1]


def planes_to_columns(value):
    top = [value[p * grid : (p + 1) * grid, :grid] for p in range(4)]
    low = [value[p * grid : (p + 1) * grid, grid:] for p in range(4)]
    return jnp.concatenate([jnp.concatenate(top, axis=1), jnp.concatenate(low, axis=1)], axis=0)


def columns_to_planes(value):
    parts = []
    for p in range(4):
        block = value[:, p * grid : (p + 1) * grid]
        parts.append(jnp.concatenate([block[:grid], block[grid:]], axis=1))
    return jnp.concatenate(parts, axis=0)


def choose(index, refs):
    value = refs[0][...]
    for at in range(1, len(refs)):
        value = jnp.where(index == at, refs[at][...], value)
    return value


def part(ref, at, rows):
    return ref[pl.ds(at * rows, rows), :]


def table_kernel(place, base, *outs):
    x, core, y, zhi, side = (place[8 + n] for n in range(5))
    at = lax.broadcasted_iota(jnp.int32, (2 * grid, 1), 0)
    goal = lax.broadcasted_iota(jnp.int32, (2 * grid, 2 * grid), 1)

    def pick(index, values):
        out = values[0]
        for n in range(1, len(values)):
            out = jnp.where(index == n, values[n], out)
        return out

    def order(index):
        return (goal == index).astype(jnp.bfloat16)

    step = at >> 5
    far = pick(step, [r for r, _ in steps])
    twin = (core + pick(step, [c for _, c in steps])) & 1

    def block(sign):
        chip = ((x + 4 + sign * far) & 3) * 2 + twin
        return ((at >> 4) & 1) * grid + chip * 16 + (at & 15)

    def planes(sign, piece):
        line = (sign * 32 * far + grid + 8 * piece + 4 * twin + ((at >> 1) & 3)) & (grid - 1)
        return (at & 1) * grid + line

    slot = (at >> 3) & 3
    staged = (zhi + 4 + pick(slot, (0, side, -side, 2))) & 3
    returned = (y + 2 + pick(slot, returns)) & 3
    line = ((at >> 6) & 3) * 32 + (((at >> 4) + 3 + side) & 3) * 8 + ((at >> 3) & 1) * 4
    row_end = ((at >> 2) & 1) * grid + line + (at & 3)
    column_end = (at & 1) * grid + line + ((at >> 1) & 3)

    def turned(left, right):
        product = lax.dot_general(
            left, right, (((1,), (1,)), ((), ())), preferred_element_type=jnp.float32
        )
        return product.astype(jnp.bfloat16)

    same = order(at)
    rows_y, columns_y = order(block(1)), order(block(-1))
    columns_x, rows_x = order(planes(-1, staged)), order(planes(1, returned))
    rows_end, columns_end = order(row_end), order(column_end)
    for half in range(2):
        forward = base[half]
        inverse = turned(same, forward)
        values = (
            inverse,
            forward,
            turned(rows_y, inverse),
            turned(inverse, columns_y),
            turned(forward, columns_x),
            turned(rows_x, forward),
            turned(rows_end, inverse),
            turned(forward, columns_end),
        )
        for out, value in zip(outs, values):
            out[half] = value


def density_kernel(first, count, place, *refs):
    targets, pairs, tables = refs[:4], refs[4 : 4 + 2 * count], refs[4 + 2 * count : 6 + 2 * count]
    kept, outs = refs[6 + 2 * count : -8], refs[-8:]
    z_table, y_table = read(tables[0]), read(tables[1])
    for earlier, out in zip(kept, outs):
        out[pl.ds(0, first * 128), :] = earlier[...]
    for at in range(count):
        band = choose(place[first + at], targets)
        packed = jnp.concatenate([band * pairs[2 * at][...], band * pairs[2 * at + 1][...]], axis=1)
        lines = product(halves(packed), z_table)
        spread = product(y_table, halves(planes_to_columns(lines)))
        for step, out in enumerate(outs):
            for p in range(4):
                out[pl.ds(((first + at) * 4 + p) * 32, 32), :] = spread[
                    step * 32 : (step + 1) * 32, p * grid : (p + 1) * grid
                ]


def convolve_kernel(weights, x_pair, xi_pair, *refs):
    arrived, outs = refs[:8], refs[8:]
    x_table, xi_table = read(x_pair), read(xi_pair)
    for pair in range(8):
        columns = [
            jnp.concatenate([ref[pl.ds(2 * pair + k, 32, 16), :] for ref in arrived], axis=0)
            for k in range(2)
        ]
        spectrum = product(x_table, halves(jnp.concatenate(columns, axis=1)))
        weight = weights[:, pl.ds(pair * 2 * grid, 2 * grid)]
        scaled = jnp.concatenate([spectrum[:grid] * weight, spectrum[grid:] * weight], axis=0)
        back = product(xi_table, halves(scaled))
        for k in range(2):
            for at, out in enumerate(outs):
                out[pl.ds(2 * pair + k, 32, 16), :] = back[
                    at * 32 : (at + 1) * 32, k * grid : (k + 1) * grid
                ]


def field_kernel(first, place, *refs):
    arrived, owns, others = refs[:8], refs[8:12], refs[12:16]
    yi_table, zi_table, outs = read(refs[16]), read(refs[17]), refs[18:]
    for at, out in enumerate(outs):
        rows = jnp.concatenate(
            [
                jnp.concatenate([part(ref, (first + at) * 4 + p, 32) for ref in arrived], axis=0)
                for p in range(4)
            ],
            axis=1,
        )
        lines = product(yi_table, halves(rows))
        values = product(halves(columns_to_planes(lines)), zi_table)
        own, other = choose(place[4 + first + at], owns), choose(place[4 + first + at], others)
        out[...] = -(own * values[:, :grid] + other * values[:, grid:])


def applied_kernel(own, one, two, three, z_pair, y_pair, out):
    applied = (own[...] + one[...]) + (two[...] + three[...])
    lines = product(halves(applied), (z_pair[0, :grid], z_pair[1, :grid]))
    spread = product(read(y_pair), halves(planes_to_columns(lines)))
    for p in range(4):
        out[:, pl.ds(p, 1)] = spread[:, p * grid : (p + 1) * grid].reshape(32, 1, 8, grid)


def mask_kernel(cells, out, plane_out, run_out):
    cell = cells[...]

    def hot(count, index):
        return lax.broadcasted_iota(jnp.int32, (count, 4096), 0) == index

    row_hot = hot(512, cell // grid).astype(jnp.bfloat16)
    lane_hot = hot(grid, cell % grid).astype(jnp.bfloat16)
    out[...] = lax.dot_general(
        row_hot, lane_hot, (((1,), (1,)), ((), ())), preferred_element_type=jnp.float32
    )
    plane_out[...] = hot(grid, cell // 512).astype(jnp.bfloat16)
    run_out[...] = hot(32, (cell // 16) % 32).astype(jnp.float32)


def pick_kernel(arrived, mask, planes, runs_at, x_pair, out):
    x_table = read(x_pair)
    lane = lax.broadcasted_iota(jnp.int32, (grid, grid), 0)
    group = lax.broadcasted_iota(jnp.int32, (grid, grid), 1)
    total = jnp.zeros((2 * grid, grid), jnp.float32)
    for pair in range(2):
        columns = [arrived[pl.ds(2 * pair + k, 2 * grid, 4), :] for k in range(2)]
        spectrum = product(x_table, halves(jnp.concatenate(columns, axis=1)))
        for k in range(2):
            row = 2 * pair + k
            kept = mask[pl.ds(row, grid, 4), :]
            part = spectrum[:, k * grid : (k + 1) * grid]
            part = jnp.concatenate([part[:grid] * kept, part[grid:] * kept], axis=0)
            ones = (group == row * 8 + lane // 16).astype(jnp.bfloat16)
            for piece in halves(part):
                total = total + lax.dot_general(
                    piece, ones, (((1,), (0,)), ((), ())), preferred_element_type=jnp.float32
                )
    norm = 1.0 / float(np.sqrt(float(grid) ** 3))
    for c in range(2):
        runs = total[c * grid : (c + 1) * grid].T[:32]
        spread = jnp.zeros((32, 4096), jnp.float32)
        for piece in halves(runs):
            spread = spread + lax.dot_general(
                piece, planes[...], (((1,), (0,)), ((), ())), preferred_element_type=jnp.float32
            )
        out[pl.ds(c, 1), :] = (
            jnp.sum(runs_at[...] * spread, axis=0, keepdims=True) * norm
        )


def call(kernel, shapes, specs, *args, flops=1 << 30):
    return pl.pallas_call(
        kernel,
        out_shape=shapes,
        in_specs=specs,
        out_specs=jax.tree.map(lambda _: vmem, shapes),
        compiler_params=params,
        cost_estimate=pl.CostEstimate(flops=flops, bytes_accessed=1 << 20, transcendentals=0),
    )(*args)


def floats(*shape):
    return jax.ShapeDtypeStruct(shape, jnp.float32)


def moved(change):
    pairs = []
    sizes = tuple(extent[a] for a in axes)
    for at in np.ndindex(sizes):
        spot = dict(zip(axes, at))
        goal = change(dict(spot))
        pairs.append((int(np.ravel_multi_index(at, sizes)),
                      int(np.ravel_multi_index(tuple(goal[a] for a in axes), sizes))))
    return pairs


def swapped(spot):
    turn = 2 * spot["zlo"]
    spot["y"], spot["zhi"] = (spot["zhi"] + 2 + turn) % 4, (spot["y"] + turn) % 4
    return spot


def swapped_back(spot):
    turn = 2 * spot["zlo"]
    spot["y"], spot["zhi"] = (spot["zhi"] + turn) % 4, (spot["y"] + 2 + turn) % 4
    return spot


def along_y(step):
    def change(spot):
        spot["y"] = (spot["y"] + step) % 4
        return spot

    return moved(change)


def along_x(step, turn):
    def change(spot):
        spot["x"] = (spot["x"] + step) % 4
        spot["core"] = (spot["core"] + turn) % 2
        return spot

    return moved(change)


def with_partner(spot):
    spot["zlo"] = 1 - spot["zlo"]
    return spot


def with_border(spot):
    z = (spot["zhi"] * 2 + spot["zlo"] + (1 if spot["zlo"] else -1)) % 8
    spot["zhi"], spot["zlo"] = z // 2, z % 2
    return spot


def send(value, pairs):
    return lax.ppermute(value, axes, pairs)


def after(value, *others):
    return lax.optimization_barrier((value,) + others)[0]


def screened_weights(first_row):
    counter = jnp.arange(grid, dtype=jnp.int32)
    folded = jnp.where(counter < grid // 2, counter, counter - grid).astype(jnp.float32)
    rows = first_row + jnp.arange(16, dtype=jnp.int32)
    folded_rows = jnp.where(rows < grid // 2, rows, rows - grid).astype(jnp.float32)
    factor = (2.0 * jnp.pi / box_length) ** 2
    square_norm = factor * (
        folded[:, None, None] ** 2 + folded_rows[None, :, None] ** 2 + folded[None, None, :] ** 2
    )
    safe_square = jnp.where(square_norm > 0, square_norm, 1.0)
    screened = 4.0 * jnp.pi / safe_square * (1.0 - jnp.exp(-safe_square / (4.0 * screening * screening)))
    kernel = jnp.where(square_norm > 0, screened, jnp.pi / (screening * screening))
    return (kernel * (1.0 / grid**3)).reshape(grid, 16 * grid)


def exchange(blocks):
    return [
        block if step == (0, 0) else send(block, along_x(*step)) for step, block in zip(steps, blocks)
    ]


def local(targets, occupied, sphere_map):
    spot = {name: lax.axis_index(name) for name in axes}
    x, y, zhi, zlo, core = (spot[name] for name in ("x", "y", "zhi", "zlo", "core"))
    side = 2 * zlo - 1
    chip = x * 2 + core
    turns = (0, side, -side, 2)
    turned = (y + 2 * zlo) % 4
    band_at = [(turned + 10 - zhi - turn) % 4 for turn in turns]
    ahead = [(turned + k + 6 - zhi) % 4 for k in returns]
    stage_at = [
        jnp.where(m == 0, 0, jnp.where(m == 2, 3, jnp.where(m == (4 + side) % 4, 1, 2))) for m in ahead
    ]
    place = jnp.stack(band_at + stage_at + [x, core, turned, zhi, side]).astype(jnp.int32)

    own = occupied.reshape(512, grid)
    partner, border = moved(with_partner), moved(with_border)
    band = send(targets.reshape(512, grid), moved(swapped))
    a1, b1 = send(own, partner), send(own, border)
    tables = call(
        table_kernel, [jax.ShapeDtypeStruct((2, 2 * grid, 2 * grid), jnp.bfloat16)] * 8,
        [smem, vmem], place, jnp.asarray(base_table()),
    )
    weights = screened_weights(chip * 16)
    a1, b1, weights, tables = lax.optimization_barrier((a1, b1, weights, tables))
    a2, b2 = send(b1, partner), send(a1, border)
    tables = dict(zip(names, tables))
    bands = [band] + [None] * 3
    for step in (2, 1, 3):
        bands[step] = send(band, along_y(step))
    a3, b3 = send(b2, partner), send(a2, border)
    a3, b3, bands[2] = lax.optimization_barrier((a3, b3, bands[2]))
    c4 = jnp.concatenate([send(b3[:256], partner), send(a3[256:], border)])
    owns, others = [own, b2, a2, c4], [a1, b1, a3, b3]

    blocks = call(
        functools.partial(density_kernel, 0, 3), [floats(384, grid)] * 8, [smem] + [vmem] * 12,
        place, *bands, own, a1, b2, b1, a2, a3, tables["z"], tables["y"],
    )
    blocks = call(
        functools.partial(density_kernel, 3, 1), [floats(512, grid)] * 8, [smem] + [vmem] * 16,
        place, *bands, c4, b3, tables["z"], tables["y"], *blocks,
    )
    arrived = exchange(blocks)
    back = call(
        convolve_kernel, [floats(512, grid)] * 8, [vmem] * 11,
        weights, tables["x"], tables["xi"], *arrived,
    )
    returned = exchange(back)
    sums = {}
    for first, count in parts:
        fields = call(
            functools.partial(field_kernel, first), [floats(512, grid)] * count, [smem] + [vmem] * 18,
            place, *returned, *owns, *others, tables["yi"], tables["zi"],
        )
        for k, field in zip(returns[first:], fields):
            sums[k] = send(field, along_y(k)) if k else field
    cells = send(after(sphere_map, sums[0]), moved(swapped)).reshape(1, 4096)
    picks = call(
        mask_kernel,
        [floats(512, grid), jax.ShapeDtypeStruct((grid, 4096), jnp.bfloat16), floats(32, 4096)],
        [vmem], cells,
    )
    sums[0], picks = lax.optimization_barrier((sums[0], picks))
    lines = call(
        applied_kernel, floats(32, 4, 8, grid), [vmem] * 6,
        *[sums[k] for k in range(4)], tables["z"], tables["y_end"],
    )
    lines = lax.all_to_all(lines, ("x", "y", "core"), 0, 0, tiled=True)
    picked = call(
        pick_kernel, floats(2, 4096), [vmem] * 5,
        lines.reshape(1024, grid), *picks, tables["x_end"],
    )
    return send(picked, moved(swapped_back))[None]


def solution(mesh):
    split = Mesh(mesh.devices.reshape(tuple(extent[a] for a in axes)), axes)
    bands, planes = ("zlo", "y"), ("x", "zhi", "core")
    return jax.shard_map(
        local,
        mesh=split,
        in_specs=(P(bands, planes, None, None), P(bands, planes, None, None), P(planes)),
        out_specs=P(bands, None, planes),
        check_vma=False,
    )
```
